32 devices in a mesh: grp: 2 (over y), wide: 4 (over z), patch: 2 (over x), sub: 2 (over core).
Axes of the slice: x: 2, y: 2, z: 4, core: 2. Of those that a mesh axis runs over, the one named last changes fastest.
Arguments:
- survey: bfloat16 [512, 20, 729], P('wide', ('grp', 'patch')), parts along dimension 1, may hold values from -34 to 34
- test_matrix: bfloat16 [625, 48], replicated, may hold values from -6 to 6
Outputs:
- restored: float32 [512, 20, 729], P('wide', ('grp', 'patch')), parts along dimension 1
The draws below stay inside these ranges and needn't reach their ends.
There are 2 independent parts, one for each index of `grp`. The reference program is written for one: setup_inputs(seed, part) draws one part's arguments, and reference() takes and returns one part's arrays. A program takes and returns all parts, laid end to end along the dimension named above; an argument that names none is the same for every part. Nothing has to cross between parts.
All inputs are finite; a program needn't handle non-finite values.
Results may differ from the reference program's by a relative error of at most 0.0014.
Values may be sent and summed in bfloat16 or wider, within the bound.
A program may use at most 64 MiB of HBM per device.

```python
import math
import jax
import jax.numpy as jnp
from jax import lax

LH = 5
RANK = 48
NT = 512
PS = 9
ORDER = 625
TR3 = 729
NF = 4
NXS = 10
N_PATCH = 2


def draw_survey(key, part):
    streams = jax.random.split(key, 6)
    moments = jnp.arange(NT, dtype=jnp.float32)[:, None, None]
    planes = jnp.arange(NXS, dtype=jnp.float32)[None, :, None]
    traces = jnp.arange(TR3, dtype=jnp.int32)
    middle = (PS - 1) / 2.0
    across_one = (traces // (PS * PS)).astype(jnp.float32)[None, None, :] - middle
    across_two = (traces // PS % PS).astype(jnp.float32)[None, None, :] - middle
    across_three = (traces % PS).astype(jnp.float32)[None, None, :] - middle
    polarity = jnp.where(jax.random.bernoulli(streams[0], 0.5, (16,)), 1.0, -1.0)
    amplitude = polarity * jax.random.uniform(streams[1], (16,), minval=0.5, maxval=1.5)
    noise_part = jnp.clip(0.7 * jax.random.normal(streams[5], (NT, NXS, TR3)), -2.8, 2.8)
    slopes = jax.random.uniform(streams[2], (16, 4), minval=-1.0, maxval=1.0)
    onsets = jax.random.uniform(streams[3], (16,), minval=0.0, maxval=float(NT))
    centres = jax.random.uniform(streams[4], (16,), minval=0.3, maxval=0.7) * (NF / NT)
    signal = noise_part
    for event_index in range(16):
        delays = moments - onsets[event_index] - slopes[event_index, 0] * planes
        delays = delays - slopes[event_index, 1] * across_one - slopes[event_index, 2] * across_two - slopes[event_index, 3] * across_three
        wrapped = jnp.mod(delays + NT / 2.0, float(NT)) - NT / 2.0
        spread = (math.pi * centres[event_index] * wrapped) ** 2
        signal = signal + amplitude[event_index] * (1.0 - 2.0 * spread) * jnp.exp(-spread)
    return signal.astype(jnp.bfloat16)


def noise(rng, dims, width, reach, kind=jnp.bfloat16):
    result = width * jax.random.normal(rng, dims, jnp.float32)
    return jnp.clip(result, min=-reach, max=reach).astype(kind)


def setup_inputs(seed: int = 0, part: int = 0) -> dict:
    key_of = jax.random.split(jax.random.key(seed), 3)
    own_keys = jax.random.split(jax.random.fold_in(key_of[2], part), 3)
    return {
        "survey": draw_survey(jax.random.fold_in(jax.random.fold_in(key_of[2], part), 71), part),
        "test_matrix": noise(key_of[1], (ORDER, RANK), 1.0, 6.0),
    }


DAMP = 0.5
HIGHEST = lax.Precision.HIGHEST

def level_weight():
    planes = jnp.arange(PS, dtype=jnp.int32)
    return jnp.minimum(jnp.minimum(planes + 1, PS - planes), LH).astype(jnp.float32)

def average_counts():
    weight = level_weight()
    return weight[:, None, None, None] * weight[None, :, None, None] * weight[None, None, :, None] * weight[None, None, None, :]

def phases(time_total, freq_total):
    frequency = jnp.arange(freq_total, dtype=jnp.int32) + 1
    moments = jnp.arange(time_total, dtype=jnp.int32)
    turned = frequency[:, None] * moments[None, :] % time_total
    return turned.astype(jnp.float32) * (2.0 * math.pi / time_total)

def forward_table(time_total, freq_total):
    angles = phases(time_total, freq_total)
    factor = 1.0 / math.sqrt(time_total)
    matrix = jnp.stack([jnp.cos(angles) * factor, -jnp.sin(angles) * factor], 1)
    return matrix.reshape(2 * freq_total, time_total).astype(jnp.bfloat16)

def inverse_table(time_total, freq_total):
    angles = phases(time_total, freq_total)
    factor = 2.0 / math.sqrt(time_total)
    matrix = jnp.stack([jnp.cos(angles) * factor, -jnp.sin(angles) * factor], 1)
    return matrix.reshape(2 * freq_total, time_total)

def spatial_fft(values):
    return jnp.fft.fftn(values, axes=(-4, -3, -2, -1))

def spatial_ifft(values):
    return jnp.fft.ifftn(values, axes=(-4, -3, -2, -1))

def padded(values):
    shaped = values.reshape(values.shape[:-1] + (LH, LH, LH, LH))
    return jnp.pad(shaped, [(0, 0)] * (shaped.ndim - 4) + [(0, LH - 1)] * 4)

def leading(values):
    corner = values[..., :LH, :LH, :LH, :LH]
    return corner.reshape(corner.shape[:-4] + (ORDER,))

def gram_of(matrix):
    return jnp.dot(matrix.astype(jnp.float32), matrix.T.astype(jnp.float32), precision=HIGHEST, preferred_element_type=jnp.float32)

def reduce_frequency(spectrum, test_hat):
    data_hat = spatial_fft(spectrum[0] + 1j * spectrum[1])
    sketch = leading(spatial_ifft(data_hat[None] * jnp.conj(test_hat)))
    real_part = jnp.real(sketch)
    imag_part = jnp.imag(sketch)
    basis_rows = jnp.concatenate([jnp.concatenate([real_part, imag_part], 1), jnp.concatenate([-imag_part, real_part], 1)], 0)
    gram_matrix = gram_of(basis_rows)
    factor = jnp.linalg.cholesky(gram_matrix)
    orthonormal = jax.scipy.linalg.solve_triangular(factor, basis_rows, lower=True).astype(jnp.bfloat16)
    orthonormal = lax.optimization_barrier(orthonormal).astype(jnp.float32)
    joined = orthonormal[:, :ORDER] + 1j * orthonormal[:, ORDER:]
    joined_hat = spatial_fft(padded(joined))
    coupled = leading(spatial_ifft(data_hat[None] * jnp.conj(joined_hat)))
    direct = jnp.real(coupled)
    twisted = -jnp.imag(coupled)
    damping = gram_of(direct) + gram_of(twisted)
    damp_level = DAMP * jnp.trace(damping) / (2 * RANK)
    shifted = damping + damp_level * jnp.eye(2 * RANK, dtype=jnp.float32)
    kernel = jax.scipy.linalg.cho_solve((jnp.linalg.cholesky(shifted), True), damping)
    coeffs = jnp.dot(kernel.astype(jnp.float32), direct.astype(jnp.float32), precision=HIGHEST, preferred_element_type=jnp.float32).astype(jnp.bfloat16)
    coeffs = lax.optimization_barrier(coeffs).astype(jnp.float32)
    summed = spatial_ifft(lax.optimization_barrier(jnp.sum(joined_hat * spatial_fft(padded(coeffs)), 0)))
    return jnp.stack([jnp.real(summed), jnp.imag(summed)], 0) / average_counts()

def reference(survey, test_matrix):
    forward = forward_table(NT, NF)
    inverse = inverse_table(NT, NF)
    test_grid = test_matrix.astype(jnp.float32).T
    test_hat = spatial_fft(padded(test_grid))
    extended = jnp.concatenate([survey, survey[:, :LH - 1, :]], 1)
    taper_weights = level_weight() / LH

    def one_patch(patch_index):
        window = lax.dynamic_slice_in_dim(extended, patch_index * LH, PS, 1)
        spectra = jnp.dot(forward.astype(jnp.float32), window.reshape(NT, PS * TR3).astype(jnp.float32), preferred_element_type=jnp.float32).astype(jnp.bfloat16)
        spectra = lax.optimization_barrier(spectra).astype(jnp.float32).reshape(NF, 2, PS, PS, PS, PS)
        averaged = lax.map(lambda spectrum: reduce_frequency(spectrum, test_hat), spectra)
        smooth = averaged.reshape(NF, 2, PS, TR3) * taper_weights[None, None, :, None]
        series = lax.dot_general(inverse.astype(jnp.float32), smooth.reshape(2 * NF, PS * TR3).astype(jnp.float32), (((0,), (0,)), ((), ())), precision=HIGHEST, preferred_element_type=jnp.float32)
        return series.reshape(NT, PS, TR3)
    patches = lax.map(one_patch, jnp.arange(N_PATCH, dtype=jnp.int32))
    carried = jnp.roll(patches[:, :, LH:, :], 1, axis=0)
    owned_planes = patches[:, :, :LH, :]
    merged = jnp.concatenate([owned_planes[:, :, :LH - 1, :] + carried, owned_planes[:, :, LH - 1:, :]], 2)
    return jnp.transpose(merged, (1, 0, 2, 3)).reshape(NT, NXS, TR3)
```

```python
import functools
import math

import jax
import jax.numpy as jnp
import numpy as np
from jax import lax
from jax.experimental import pallas as pl
from jax.experimental.pallas import tpu as pltpu
from jax.sharding import PartitionSpec as P

LH = 5
RANK = 48
FD = 1
PS = 9
TR3 = 729
INNER = LH * LH
PLANE = PS * PS
DAMP = 0.5
HIGHEST = lax.Precision.HIGHEST
LANES = 128
HALF = 64
SPAN = LH * LANES
QROWS = 32


def level_weight():
    planes = np.arange(PS)
    return np.minimum(np.minimum(planes + 1, PS - planes), LH).astype(np.float32)


def phases(time_total, freq_total):
    frequency = jnp.arange(freq_total, dtype=jnp.int32) + 1
    moments = jnp.arange(time_total, dtype=jnp.int32)
    turned = frequency[:, None] * moments[None, :] % time_total
    return turned.astype(jnp.float32) * (2.0 * math.pi / time_total)


def forward_table(time_total, freq_total):
    angles = phases(time_total, freq_total)
    factor = 1.0 / math.sqrt(time_total)
    matrix = jnp.stack([jnp.cos(angles) * factor, -jnp.sin(angles) * factor], 1)
    return matrix.reshape(2 * freq_total, time_total).astype(jnp.bfloat16)


def inverse_table(time_total, freq_total):
    angles = phases(time_total, freq_total)
    factor = 2.0 / math.sqrt(time_total)
    matrix = jnp.stack([jnp.cos(angles) * factor, -jnp.sin(angles) * factor], 1)
    return matrix.reshape(2 * freq_total, time_total)


def picker():
    table = np.zeros((SPAN, LANES), np.float32)
    for b in range(LH):
        for c in range(LH):
            for d in range(LH):
                table[b * LANES + c * PS + d, b * INNER + c * LH + d] = 1.0
    return table


def scale_table():
    w = level_weight()
    taper = w / LH
    full = taper[None, :, None, None] / (
        w[:, None, None, None] * w[None, :, None, None] * w[None, None, :, None] * w[None, None, None, :]
    )
    full = full.reshape(PS, PS, PLANE)
    both = np.concatenate([full, full], 1)
    return np.pad(both, ((0, 0), (0, 0), (0, LANES - PLANE))).astype(np.float32)


def eliminate(matrix, full):
    groups = RANK // 8
    lane = lax.broadcasted_iota(jnp.int32, (8, LANES), 1)
    sub = lax.broadcasted_iota(jnp.int32, (8, LANES), 0)
    sign = jnp.where(lax.broadcasted_iota(jnp.int32, (1, LANES), 1) < HALF, -1.0, 1.0)
    x = [matrix[8 * g : 8 * g + 8] for g in range(groups)]
    w = [jnp.where(lane == sub + 8 * g, 1.0, 0.0) for g in range(groups)]
    inverses = []
    for k in range(RANK):
        home, at = divmod(k, 8)
        row_x = x[home][at : at + 1]
        row_w = w[home][at : at + 1]
        inv = 1.0 / row_x[:, k : k + 1]
        inverses.append(inv)
        row_x = row_x * inv
        row_w = row_w * inv
        turn_x = pltpu.roll(row_x, HALF, 1) * sign
        turn_w = pltpu.roll(row_w, HALF, 1) * sign
        for g in range(groups):
            if not full and g < home:
                continue
            m_re = x[g][:, k : k + 1]
            m_im = x[g][:, HALF + k : HALF + k + 1]
            new_x = x[g] - (m_re * row_x + m_im * turn_x)
            new_w = w[g] - (m_re * row_w + m_im * turn_w)
            if g == home:
                keep = sub == at if full else sub <= at
                new_x = jnp.where(keep, x[g], new_x)
                new_w = jnp.where(keep, w[g], new_w)
            x[g] = new_x
            w[g] = new_w
    scale = []
    for g in range(groups):
        column = jnp.zeros((8, 1), jnp.float32)
        rows = lax.broadcasted_iota(jnp.int32, (8, 1), 0)
        for at in range(8):
            column = jnp.where(rows == at, inverses[8 * g + at], column)
        scale.append(column if full else jnp.sqrt(column))
    return jnp.concatenate([w[g] * scale[g] for g in range(groups)], 0)


def hermitian(left, re, im):
    gap = jnp.zeros((HALF - RANK, 2 * SPAN), jnp.float32)
    right = jnp.concatenate([re, gap, im, gap], 0)
    return lax.dot_general(
        left, right, (((1,), (1,)), ((), ())), precision=HIGHEST, preferred_element_type=jnp.float32
    )


def spread(left, top, bottom):
    gap = jnp.zeros((HALF - RANK, 2 * SPAN), jnp.float32)
    right = jnp.concatenate([top, gap, bottom, gap], 0)
    return jnp.dot(left, right, precision=HIGHEST, preferred_element_type=jnp.float32)


def frequency_kernel(x_ref, test_ref, pick_ref, pick_t_ref, scale_ref, out_ref, t_ref, y_ref, h_ref):
    rows_ea = 2 * PS
    t_ref[...] = jnp.zeros_like(t_ref)
    for q in range(INNER):
        off = q // LH * PS + q % LH
        for big in range(PS):
            piece = x_ref[big]
            if off:
                piece = pltpu.roll(piece, LANES - off, 1)
            t_ref[big, pl.ds(q, rows_ea, stride=QROWS), :] = piece
    y_ref[...] = jnp.zeros_like(y_ref)
    pick = pick_ref[...]
    part = PS * QROWS
    for e in range(2):
        for b in range(LH):
            block = jnp.concatenate(
                [t_ref[b + s, e * part : (e + 1) * part, :].astype(jnp.bfloat16) for s in range(LH)], 1
            )
            got = jnp.dot(block, pick, preferred_element_type=jnp.float32)
            for big in range(PS):
                y_ref[
                    big * LANES + b * INNER : big * LANES + (b + 1) * INNER, e * LANES : (e + 1) * LANES
                ] = got[big * QROWS : big * QROWS + INNER]
    h_ref[...] = y_ref[: PS * LANES, :].astype(jnp.bfloat16)

    def times_hankel(left):
        outs = [
            jnp.dot(left, h_ref[a * LANES : a * LANES + SPAN, :], preferred_element_type=jnp.float32)
            for a in range(LH)
        ]
        re = jnp.concatenate([o[:, :LANES] for o in outs], 1)
        im = jnp.concatenate([o[:, LANES:] for o in outs], 1)
        return re, im

    p_re, p_im = times_hankel(test_ref[...])
    straight = jnp.concatenate([p_re, p_im], 1)
    crossed = jnp.concatenate([p_im, -p_re], 1)
    gram = hermitian(straight, straight, crossed)
    root = eliminate(gram, False)
    ortho = spread(root, jnp.concatenate([p_re, -p_im], 1), jnp.concatenate([p_im, p_re], 1))
    gap = jnp.zeros((HALF - RANK, SPAN), jnp.float32)
    q_rows = jnp.concatenate([ortho[:, :SPAN], gap, ortho[:, SPAN:], gap], 0)
    q_left = q_rows.astype(jnp.bfloat16)
    mixed_re, mixed_im = times_hankel(q_left)
    c_re = mixed_re[:RANK] - mixed_im[HALF : HALF + RANK]
    c_im = mixed_im[:RANK] + mixed_re[HALF : HALF + RANK]
    coupled = jnp.concatenate([c_re, c_im], 1)
    damping = hermitian(coupled, coupled, jnp.concatenate([-c_im, c_re], 1))
    lane = lax.broadcasted_iota(jnp.int32, (RANK, LANES), 1)
    row = lax.broadcasted_iota(jnp.int32, (RANK, LANES), 0)
    diagonal = lane == row
    level = DAMP * jnp.sum(jnp.where(diagonal, damping, 0.0)) / RANK
    solved = eliminate(damping + jnp.where(diagonal, level, 0.0), True)
    coeffs = coupled - level * spread(solved, coupled, jnp.concatenate([-c_im, c_re], 1))
    f_re = coeffs[:, :SPAN].astype(jnp.bfloat16)
    f_im = coeffs[:, SPAN:].astype(jnp.bfloat16)
    gap16 = jnp.zeros((HALF - RANK, LANES), jnp.bfloat16)
    q_t = jnp.transpose(q_rows).astype(jnp.bfloat16)
    y_ref[...] = jnp.zeros_like(y_ref)
    for a in range(LH):
        at = slice(a * LANES, (a + 1) * LANES)
        left = jnp.concatenate([f_re[:, at], gap16, f_im[:, at], gap16], 0)
        right = jnp.concatenate([f_im[:, at], gap16, -f_re[:, at], gap16], 0)
        y_ref[a * LANES : a * LANES + SPAN, :] += jnp.dot(
            q_t, jnp.concatenate([left, right], 1), preferred_element_type=jnp.float32
        )
    t_ref[...] = jnp.zeros_like(t_ref)
    pick_t = pick_t_ref[...]
    for e in range(2):
        for b in range(LH):
            lines = jnp.concatenate(
                [
                    y_ref[
                        big * LANES + b * INNER : big * LANES + b * INNER + QROWS,
                        e * LANES : (e + 1) * LANES,
                    ]
                    for big in range(PS)
                ],
                0,
            )
            high = lines.astype(jnp.bfloat16)
            low = (lines - high.astype(jnp.float32)).astype(jnp.bfloat16)
            wide_lines = jnp.dot(
                jnp.concatenate([high, low], 1), pick_t, preferred_element_type=jnp.float32
            )
            for s in range(LH):
                t_ref[b + s, e * part : (e + 1) * part, :] += wide_lines[:, s * LANES : (s + 1) * LANES]
    for big in range(PS):
        total = jnp.zeros((rows_ea, LANES), jnp.float32)
        for q in range(INNER):
            off = q // LH * PS + q % LH
            piece = t_ref[big, pl.ds(q, rows_ea, stride=QROWS), :]
            total = total + (pltpu.roll(piece, off, 1) if off else piece)
        out_ref[big] = total * scale_ref[big]


def reduce_frequency(spectrum, test_rows):
    laid = jnp.transpose(spectrum, (2, 0, 1, 3)).reshape(PS, 2 * PS, PLANE)
    laid = jnp.pad(laid, ((0, 0), (0, 0), (0, LANES - PLANE)))
    pick = picker()
    pick_t = np.concatenate([pick.T, pick.T], 0)
    out = pl.pallas_call(
        frequency_kernel,
        out_shape=jax.ShapeDtypeStruct((PS, 2 * PS, LANES), jnp.float32),
        in_specs=[pl.BlockSpec(memory_space=pltpu.VMEM)] * 5,
        out_specs=pl.BlockSpec(memory_space=pltpu.VMEM),
        scratch_shapes=[
            pltpu.VMEM((PS, 2 * PS * QROWS, LANES), jnp.float32),
            pltpu.VMEM((PS * LANES + 8, 2 * LANES), jnp.float32),
            pltpu.VMEM((PS * LANES, 2 * LANES), jnp.bfloat16),
        ],
        compiler_params=pltpu.CompilerParams(vmem_limit_bytes=40 * 1024 * 1024),
    )(
        laid,
        test_rows,
        jnp.asarray(pick, jnp.bfloat16),
        jnp.asarray(pick_t, jnp.bfloat16),
        jnp.asarray(scale_table()),
    )
    return jnp.transpose(out[:, :, :PLANE].reshape(PS, 2, PS, PLANE), (1, 2, 0, 3)).reshape(2, PS, TR3)


def shift_patch(x, by):
    devices = lax.axis_size("patch")
    return lax.ppermute(x, "patch", [(i, (i + by) % devices) for i in range(devices)])


def shards(survey, test_matrix):
    wide_count = lax.axis_size("wide")
    mine = lax.axis_index("wide")
    time_local, plane_count, unused_size = survey.shape
    time_total = time_local * wide_count
    freq_total = FD * wide_count
    forward = forward_table(time_total, freq_total)
    own_forward = lax.dynamic_slice_in_dim(forward, mine * time_local, time_local, 1)
    partial = jnp.dot(
        own_forward, survey.reshape(time_local, plane_count * TR3), preferred_element_type=jnp.float32
    )
    partial = partial.reshape(wide_count, 2 * FD * plane_count * TR3)
    pieces = lax.all_to_all(partial, "wide", split_axis=0, concat_axis=0, tiled=True)
    spectra = jnp.sum(pieces, 0).astype(jnp.bfloat16).reshape(FD, 2, plane_count, TR3)
    rim = shift_patch(spectra[:, :, : LH - 1], -1)
    grid = jnp.concatenate([spectra, rim], 2).astype(jnp.float32)
    test_rows = jnp.pad(
        test_matrix.T.reshape(RANK, LH, LH * INNER), ((0, 0), (0, 0), (0, LANES - LH * INNER))
    ).reshape(RANK, SPAN)
    smooth = jnp.stack([reduce_frequency(grid[f].reshape(2, PS, PS, PLANE), test_rows) for f in range(FD)], 0)
    carried = shift_patch(smooth[:, :, LH:, :], 1)
    smooth = jnp.concatenate([smooth[:, :, : LH - 1, :] + carried, smooth[:, :, LH - 1 : LH, :]], 2)
    gathered = lax.all_gather(smooth.reshape(2 * FD, plane_count * TR3), "wide", axis=0, tiled=True)
    inverse = inverse_table(time_total, freq_total)
    own_inverse = lax.dynamic_slice_in_dim(inverse, mine * time_local, time_local, 1)
    series = lax.dot_general(
        own_inverse, gathered, (((0,), (0,)), ((), ())), precision=HIGHEST, preferred_element_type=jnp.float32
    )
    return series.reshape(time_local, plane_count, TR3)


def solution(mesh):
    return jax.shard_map(
        shards,
        mesh=mesh,
        in_specs=(P("wide", ("grp", "patch"), None), P()),
        out_specs=P("wide", ("grp", "patch"), None),
        check_vma=False,
    )
```

```python
import functools
import math

import jax
import jax.numpy as jnp
import numpy as np
from jax import lax
from jax.experimental import pallas as pl
from jax.experimental.pallas import tpu as pltpu
from jax.sharding import PartitionSpec as P

LH = 5
RANK = 48
FD = 1
PS = 9
TR3 = 729
INNER = LH * LH
PLANE = PS * PS
DAMP = 0.5
HIGHEST = lax.Precision.HIGHEST
LANES = 128
HALF = 64
SPAN = LH * LANES
QROWS = 32


def level_weight():
    planes = np.arange(PS)
    return np.minimum(np.minimum(planes + 1, PS - planes), LH).astype(np.float32)


def phases(time_total, freq_total):
    frequency = jnp.arange(freq_total, dtype=jnp.int32) + 1
    moments = jnp.arange(time_total, dtype=jnp.int32)
    turned = frequency[:, None] * moments[None, :] % time_total
    return turned.astype(jnp.float32) * (2.0 * math.pi / time_total)


def forward_table(time_total, freq_total):
    angles = phases(time_total, freq_total)
    factor = 1.0 / math.sqrt(time_total)
    matrix = jnp.stack([jnp.cos(angles) * factor, -jnp.sin(angles) * factor], 1)
    return matrix.reshape(2 * freq_total, time_total).astype(jnp.bfloat16)


def inverse_table(time_total, freq_total):
    angles = phases(time_total, freq_total)
    factor = 2.0 / math.sqrt(time_total)
    matrix = jnp.stack([jnp.cos(angles) * factor, -jnp.sin(angles) * factor], 1)
    return matrix.reshape(2 * freq_total, time_total)


def picker():
    table = np.zeros((SPAN, LANES), np.float32)
    for b in range(LH):
        for c in range(LH):
            for d in range(LH):
                table[b * LANES + c * PS + d, b * INNER + c * LH + d] = 1.0
    return table


def scale_table():
    w = level_weight()
    taper = w / LH
    full = taper[None, :, None, None] / (
        w[:, None, None, None] * w[None, :, None, None] * w[None, None, :, None] * w[None, None, None, :]
    )
    full = full.reshape(PS, PS, PLANE)
    both = np.concatenate([full, full], 1)
    return np.pad(both, ((0, 0), (0, 0), (0, LANES - PLANE))).astype(np.float32)


def eliminate(matrix, full):
    groups = RANK // 8
    lane = lax.broadcasted_iota(jnp.int32, (8, LANES), 1)
    sub = lax.broadcasted_iota(jnp.int32, (8, LANES), 0)
    sign = jnp.where(lax.broadcasted_iota(jnp.int32, (1, LANES), 1) < HALF, -1.0, 1.0)
    x = [matrix[8 * g : 8 * g + 8] for g in range(groups)]
    w = [jnp.where(lane == sub + 8 * g, 1.0, 0.0) for g in range(groups)]
    inverses = []
    for k in range(RANK):
        home, at = divmod(k, 8)
        row_x = x[home][at : at + 1]
        row_w = w[home][at : at + 1]
        inv = 1.0 / row_x[:, k : k + 1]
        inverses.append(inv)
        row_x = row_x * inv
        row_w = row_w * inv
        turn_x = pltpu.roll(row_x, HALF, 1) * sign
        turn_w = pltpu.roll(row_w, HALF, 1) * sign
        for g in range(groups):
            if not full and g < home:
                continue
            m_re = x[g][:, k : k + 1]
            m_im = x[g][:, HALF + k : HALF + k + 1]
            new_x = x[g] - (m_re * row_x + m_im * turn_x)
            new_w = w[g] - (m_re * row_w + m_im * turn_w)
            if g == home:
                keep = sub == at if full else sub <= at
                new_x = jnp.where(keep, x[g], new_x)
                new_w = jnp.where(keep, w[g], new_w)
            x[g] = new_x
            w[g] = new_w
    scale = []
    for g in range(groups):
        column = jnp.zeros((8, 1), jnp.float32)
        rows = lax.broadcasted_iota(jnp.int32, (8, 1), 0)
        for at in range(8):
            column = jnp.where(rows == at, inverses[8 * g + at], column)
        scale.append(column if full else jnp.sqrt(column))
    return jnp.concatenate([w[g] * scale[g] for g in range(groups)], 0)


def hermitian(left, re, im):
    gap = jnp.zeros((HALF - RANK, 2 * SPAN), jnp.float32)
    right = jnp.concatenate([re, gap, im, gap], 0)
    return lax.dot_general(
        left, right, (((1,), (1,)), ((), ())), precision=HIGHEST, preferred_element_type=jnp.float32
    )


def spread(left, top, bottom):
    gap = jnp.zeros((HALF - RANK, 2 * SPAN), jnp.float32)
    right = jnp.concatenate([top, gap, bottom, gap], 0)
    return jnp.dot(left, right, precision=HIGHEST, preferred_element_type=jnp.float32)


def frequency_kernel(x_ref, test_ref, pick_ref, pick_t_ref, scale_ref, out_ref, t_ref, y_ref, h_ref):
    rows_ea = 2 * PS
    t_ref[...] = jnp.zeros_like(t_ref)
    for q in range(INNER):
        off = q // LH * PS + q % LH
        for big in range(PS):
            piece = x_ref[big]
            if off:
                piece = pltpu.roll(piece, LANES - off, 1)
            t_ref[big, pl.ds(q, rows_ea, stride=QROWS), :] = piece
    y_ref[...] = jnp.zeros_like(y_ref)
    pick = pick_ref[...]
    part = PS * QROWS
    for e in range(2):
        for b in range(LH):
            block = jnp.concatenate(
                [t_ref[b + s, e * part : (e + 1) * part, :].astype(jnp.bfloat16) for s in range(LH)], 1
            )
            got = jnp.dot(block, pick, preferred_element_type=jnp.float32)
            for big in range(PS):
                y_ref[
                    big * LANES + b * INNER : big * LANES + (b + 1) * INNER, e * LANES : (e + 1) * LANES
                ] = got[big * QROWS : big * QROWS + INNER]
    h_ref[...] = y_ref[: PS * LANES, :].astype(jnp.bfloat16)

    def times_hankel(left):
        outs = [
            jnp.dot(left, h_ref[a * LANES : a * LANES + SPAN, :], preferred_element_type=jnp.float32)
            for a in range(LH)
        ]
        re = jnp.concatenate([o[:, :LANES] for o in outs], 1)
        im = jnp.concatenate([o[:, LANES:] for o in outs], 1)
        return re, im

    p_re, p_im = times_hankel(test_ref[...])
    straight = jnp.concatenate([p_re, p_im], 1)
    crossed = jnp.concatenate([p_im, -p_re], 1)
    gram = hermitian(straight, straight, crossed)
    root = eliminate(gram, False)
    ortho = spread(root, jnp.concatenate([p_re, -p_im], 1), jnp.concatenate([p_im, p_re], 1))
    gap = jnp.zeros((HALF - RANK, SPAN), jnp.float32)
    q_rows = jnp.concatenate([ortho[:, :SPAN], gap, ortho[:, SPAN:], gap], 0)
    q_left = q_rows.astype(jnp.bfloat16)
    mixed_re, mixed_im = times_hankel(q_left)
    c_re = mixed_re[:RANK] - mixed_im[HALF : HALF + RANK]
    c_im = mixed_im[:RANK] + mixed_re[HALF : HALF + RANK]
    coupled = jnp.concatenate([c_re, c_im], 1)
    damping = hermitian(coupled, coupled, jnp.concatenate([-c_im, c_re], 1))
    lane = lax.broadcasted_iota(jnp.int32, (RANK, LANES), 1)
    row = lax.broadcasted_iota(jnp.int32, (RANK, LANES), 0)
    diagonal = lane == row
    level = DAMP * jnp.sum(jnp.where(diagonal, damping, 0.0)) / RANK
    solved = eliminate(damping + jnp.where(diagonal, level, 0.0), True)
    coeffs = coupled - level * spread(solved, coupled, jnp.concatenate([-c_im, c_re], 1))
    f_re = coeffs[:, :SPAN].astype(jnp.bfloat16)
    f_im = coeffs[:, SPAN:].astype(jnp.bfloat16)
    gap16 = jnp.zeros((HALF - RANK, LANES), jnp.bfloat16)
    q_t = jnp.transpose(q_rows).astype(jnp.bfloat16)
    y_ref[...] = jnp.zeros_like(y_ref)
    for a in range(LH):
        at = slice(a * LANES, (a + 1) * LANES)
        left = jnp.concatenate([f_re[:, at], gap16, f_im[:, at], gap16], 0)
        right = jnp.concatenate([f_im[:, at], gap16, -f_re[:, at], gap16], 0)
        y_ref[a * LANES : a * LANES + SPAN, :] += jnp.dot(
            q_t, jnp.concatenate([left, right], 1), preferred_element_type=jnp.float32
        )
    t_ref[...] = jnp.zeros_like(t_ref)
    pick_t = pick_t_ref[...]
    for e in range(2):
        for b in range(LH):
            lines = jnp.concatenate(
                [
                    y_ref[
                        big * LANES + b * INNER : big * LANES + b * INNER + QROWS,
                        e * LANES : (e + 1) * LANES,
                    ]
                    for big in range(PS)
                ],
                0,
            )
            high = lines.astype(jnp.bfloat16)
            low = (lines - high.astype(jnp.float32)).astype(jnp.bfloat16)
            wide_lines = jnp.dot(
                jnp.concatenate([high, low], 1), pick_t, preferred_element_type=jnp.float32
            )
            for s in range(LH):
                t_ref[b + s, e * part : (e + 1) * part, :] += wide_lines[:, s * LANES : (s + 1) * LANES]
    for big in range(PS):
        total = jnp.zeros((rows_ea, LANES), jnp.float32)
        for q in range(INNER):
            off = q // LH * PS + q % LH
            piece = t_ref[big, pl.ds(q, rows_ea, stride=QROWS), :]
            total = total + (pltpu.roll(piece, off, 1) if off else piece)
        out_ref[big] = total * scale_ref[big]


def reduce_frequency(spectrum, test_rows):
    laid = jnp.transpose(spectrum, (2, 0, 1, 3)).reshape(PS, 2 * PS, PLANE)
    laid = jnp.pad(laid, ((0, 0), (0, 0), (0, LANES - PLANE)))
    pick = picker()
    pick_t = np.concatenate([pick.T, pick.T], 0)
    out = pl.pallas_call(
        frequency_kernel,
        name="frequency",
        out_shape=jax.ShapeDtypeStruct((PS, 2 * PS, LANES), jnp.float32),
        in_specs=[pl.BlockSpec(memory_space=pltpu.VMEM)] * 5,
        out_specs=pl.BlockSpec(memory_space=pltpu.VMEM),
        scratch_shapes=[
            pltpu.VMEM((PS, 2 * PS * QROWS, LANES), jnp.float32),
            pltpu.VMEM((PS * LANES + 8, 2 * LANES), jnp.float32),
            pltpu.VMEM((PS * LANES, 2 * LANES), jnp.bfloat16),
        ],
        compiler_params=pltpu.CompilerParams(vmem_limit_bytes=40 * 1024 * 1024),
    )(
        laid,
        test_rows,
        jnp.asarray(pick, jnp.bfloat16),
        jnp.asarray(pick_t, jnp.bfloat16),
        jnp.asarray(scale_table()),
    )
    return jnp.transpose(out[:, :, :PLANE].reshape(PS, 2, PS, PLANE), (1, 2, 0, 3)).reshape(2, PS, TR3)


def exchange(by, full_ref, edge_ref, own, far, send, recv):
    count = lax.axis_size("wide")
    patches = lax.axis_size("patch")
    mine = lax.axis_index("wide")
    here = lax.axis_index("patch")
    target_patch = lax.rem(here + by + patches, patches)
    source_patch = lax.rem(here - by + patches, patches)
    barrier = pltpu.get_barrier_semaphore()
    for k in range(count):
        other = lax.rem(mine + k, count)
        if k:
            pl.semaphore_signal(barrier, inc=1, device_id={"wide": other}, device_id_type=pl.DeviceIdType.MESH)
        pl.semaphore_signal(
            barrier,
            inc=1,
            device_id={"wide": other, "patch": source_patch},
            device_id_type=pl.DeviceIdType.MESH,
        )
    pl.semaphore_wait(barrier, 2 * count - 1)

    def block(ref, index):
        return ref.at[0] if ref.shape[0] == 1 else ref.at[index]

    def full_copy(target, slot):
        return pltpu.make_async_remote_copy(
            src_ref=block(full_ref, target),
            dst_ref=own.at[slot],
            send_sem=send.at[0, target],
            recv_sem=recv.at[0, slot],
            device_id={"wide": target},
            device_id_type=pl.DeviceIdType.MESH,
        )

    def edge_copy(target, slot):
        return pltpu.make_async_remote_copy(
            src_ref=block(edge_ref, target),
            dst_ref=far.at[slot],
            send_sem=send.at[1, target],
            recv_sem=recv.at[1, slot],
            device_id={"wide": target, "patch": target_patch},
            device_id_type=pl.DeviceIdType.MESH,
        )

    order = list(range(count - 1, -1, -1))
    for k in order:
        target = lax.rem(mine + k, count)
        if k:
            full_copy(target, mine).start()
        edge_copy(target, mine).start()
    own[mine] = block(full_ref, mine)[...]
    for k in order:
        source = lax.rem(mine + count - k, count)
        if k:
            full_copy(source, source).wait_recv()
        edge_copy(source, source).wait_recv()
    for k in order:
        target = lax.rem(mine + k, count)
        if k:
            full_copy(target, mine).wait_send()
        edge_copy(target, mine).wait_send()


def collect_kernel(full_ref, edge_ref, own_out, far_out, own, far, send, recv):
    exchange(-1, full_ref, edge_ref, own, far, send, recv)
    own_out[...] = jnp.sum(own[...], 0).astype(jnp.bfloat16).astype(jnp.float32)
    far_out[...] = jnp.sum(far[...], 0).astype(jnp.bfloat16).astype(jnp.float32)


def share_kernel(full_ref, edge_ref, out_ref, own, far, send, recv):
    exchange(1, full_ref, edge_ref, own, far, send, recv)
    width = far.shape[-1]
    out_ref[...] = own[...]
    out_ref[:, :, :width] = own[:, :, :width] + far[...]


def exchange_call(kernel, name, full, edge, outs, identity):
    count = lax.axis_size("wide")
    shapes = [(count,) + full.shape[1:], (count,) + edge.shape[1:]]
    return pl.pallas_call(
        kernel,
        name=name,
        out_shape=[jax.ShapeDtypeStruct(o, jnp.float32) for o in outs],
        in_specs=[pl.BlockSpec(memory_space=pltpu.VMEM)] * 2,
        out_specs=[pl.BlockSpec(memory_space=pltpu.VMEM)] * len(outs),
        scratch_shapes=[
            pltpu.VMEM(shapes[0], jnp.float32),
            pltpu.VMEM(shapes[1], jnp.float32),
            pltpu.SemaphoreType.DMA((2, count)),
            pltpu.SemaphoreType.DMA((2, count)),
        ],
        compiler_params=pltpu.CompilerParams(
            collective_id=identity, has_side_effects=True, vmem_limit_bytes=40 * 1024 * 1024
        ),
    )(full, edge)


def shards(survey, test_matrix):
    wide_count = lax.axis_size("wide")
    mine = lax.axis_index("wide")
    time_local, plane_count, unused_size = survey.shape
    time_total = time_local * wide_count
    freq_total = FD * wide_count
    traces = plane_count * TR3
    margin = (LH - 1) * TR3
    forward = forward_table(time_total, freq_total)
    own_forward = lax.dynamic_slice_in_dim(forward, mine * time_local, time_local, 1)
    partial = jnp.dot(own_forward, survey.reshape(time_local, traces), preferred_element_type=jnp.float32)
    partial = partial.reshape(wide_count, 2 * FD, traces)
    spectra, rim = exchange_call(
        collect_kernel, "collect", partial, partial[:, :, :margin], [(2 * FD, traces), (2 * FD, margin)], 0
    )
    grid = jnp.concatenate([spectra, rim], 1).reshape(FD, 2, PS, PS, PLANE)
    test_rows = jnp.pad(
        test_matrix.T.reshape(RANK, LH, LH * INNER), ((0, 0), (0, 0), (0, LANES - LH * INNER))
    ).reshape(RANK, SPAN)
    smooth = jnp.stack([reduce_frequency(grid[f], test_rows) for f in range(FD)], 0)
    smooth = smooth.reshape(1, 2 * FD, PS * TR3)
    (gathered,) = exchange_call(
        share_kernel,
        "share",
        smooth[:, :, :traces],
        smooth[:, :, traces:],
        [(wide_count, 2 * FD, traces)],
        1,
    )
    inverse = inverse_table(time_total, freq_total)
    own_inverse = lax.dynamic_slice_in_dim(inverse, mine * time_local, time_local, 1)
    series = lax.dot_general(
        own_inverse,
        gathered.reshape(2 * freq_total, traces),
        (((0,), (0,)), ((), ())),
        precision=HIGHEST,
        preferred_element_type=jnp.float32,
    )
    return series.reshape(time_local, plane_count, TR3)


def solution(mesh):
    return jax.shard_map(
        shards,
        mesh=mesh,
        in_specs=(P("wide", ("grp", "patch"), None), P()),
        out_specs=P("wide", ("grp", "patch"), None),
        check_vma=False,
    )
```

```python
import functools
import math

import jax
import jax.numpy as jnp
import numpy as np
from jax import lax
from jax.experimental import pallas as pl
from jax.experimental.pallas import tpu as pltpu
from jax.sharding import PartitionSpec as P

LH = 5
RANK = 48
FD = 1
PS = 9
TR3 = 729
INNER = LH * LH
PLANE = PS * PS
DAMP = 0.5
HIGHEST = lax.Precision.HIGHEST
LANES = 128
HALF = 64
SPAN = LH * LANES
QROWS = 32


def level_weight():
    planes = np.arange(PS)
    return np.minimum(np.minimum(planes + 1, PS - planes), LH).astype(np.float32)


def phases(time_total, freq_total):
    frequency = jnp.arange(freq_total, dtype=jnp.int32) + 1
    moments = jnp.arange(time_total, dtype=jnp.int32)
    turned = frequency[:, None] * moments[None, :] % time_total
    return turned.astype(jnp.float32) * (2.0 * math.pi / time_total)


def forward_table(time_total, freq_total):
    angles = phases(time_total, freq_total)
    factor = 1.0 / math.sqrt(time_total)
    matrix = jnp.stack([jnp.cos(angles) * factor, -jnp.sin(angles) * factor], 1)
    return matrix.reshape(2 * freq_total, time_total).astype(jnp.bfloat16)


def inverse_table(time_total, freq_total):
    angles = phases(time_total, freq_total)
    factor = 2.0 / math.sqrt(time_total)
    matrix = jnp.stack([jnp.cos(angles) * factor, -jnp.sin(angles) * factor], 1)
    return matrix.reshape(2 * freq_total, time_total)


def picker():
    table = np.zeros((SPAN, LANES), np.float32)
    for b in range(LH):
        for c in range(LH):
            for d in range(LH):
                table[b * LANES + c * PS + d, b * INNER + c * LH + d] = 1.0
    return table


def scale_table():
    w = level_weight()
    taper = w / LH
    full = taper[None, :, None, None] / (
        w[:, None, None, None] * w[None, :, None, None] * w[None, None, :, None] * w[None, None, None, :]
    )
    full = full.reshape(PS, PS, PLANE)
    both = np.concatenate([full, full], 1)
    return np.pad(both, ((0, 0), (0, 0), (0, LANES - PLANE))).astype(np.float32)


def eliminate(matrix, full):
    groups = RANK // 8
    lane = lax.broadcasted_iota(jnp.int32, (8, LANES), 1)
    sub = lax.broadcasted_iota(jnp.int32, (8, LANES), 0)
    sign = jnp.where(lax.broadcasted_iota(jnp.int32, (1, LANES), 1) < HALF, -1.0, 1.0)
    x = [matrix[8 * g : 8 * g + 8] for g in range(groups)]
    w = [jnp.where(lane == sub + 8 * g, 1.0, 0.0) for g in range(groups)]
    inverses = []
    for k in range(RANK):
        home, at = divmod(k, 8)
        row_x = x[home][at : at + 1]
        row_w = w[home][at : at + 1]
        first = 0 if full else home
        m_re = {g: jnp.broadcast_to(x[g][:, k : k + 1], (8, LANES)) for g in range(first, groups)}
        m_im = {
            g: jnp.broadcast_to(x[g][:, HALF + k : HALF + k + 1], (8, LANES)) for g in range(first, groups)
        }
        turn_x = pltpu.roll(row_x, HALF, 1) * sign
        turn_w = pltpu.roll(row_w, HALF, 1) * sign
        inv = 1.0 / m_re[home][at : at + 1]
        inverses.append(inv)
        row_x = row_x * inv
        row_w = row_w * inv
        turn_x = turn_x * inv
        turn_w = turn_w * inv
        for g in range(first, groups):
            new_x = x[g] - (m_re[g] * row_x + m_im[g] * turn_x)
            new_w = w[g] - (m_re[g] * row_w + m_im[g] * turn_w)
            if g == home:
                keep = sub == at if full else sub <= at
                new_x = jnp.where(keep, x[g], new_x)
                new_w = jnp.where(keep, w[g], new_w)
            x[g] = new_x
            w[g] = new_w
    scale = []
    for g in range(groups):
        column = jnp.zeros((8, LANES), jnp.float32)
        for at in range(8):
            column = jnp.where(sub == at, inverses[8 * g + at], column)
        scale.append(column if full else jnp.sqrt(column))
    return jnp.concatenate([w[g] * scale[g] for g in range(groups)], 0)


def hermitian(left, re, im):
    gap = jnp.zeros((HALF - RANK, 2 * SPAN), jnp.float32)
    right = jnp.concatenate([re, gap, im, gap], 0)
    return lax.dot_general(
        left, right, (((1,), (1,)), ((), ())), precision=HIGHEST, preferred_element_type=jnp.float32
    )


def spread(left, top, bottom):
    gap = jnp.zeros((HALF - RANK, 2 * SPAN), jnp.float32)
    right = jnp.concatenate([top, gap, bottom, gap], 0)
    return jnp.dot(left, right, precision=HIGHEST, preferred_element_type=jnp.float32)


def frequency_kernel(x_ref, test_ref, pick_ref, pick_t_ref, scale_ref, out_ref, t_ref, y_ref, h_ref):
    rows_ea = 2 * PS
    t_ref[...] = jnp.zeros_like(t_ref)
    for q in range(INNER):
        off = q // LH * PS + q % LH
        for big in range(PS):
            piece = x_ref[big]
            if off:
                piece = pltpu.roll(piece, LANES - off, 1)
            t_ref[big, pl.ds(q, rows_ea, stride=QROWS), :] = piece
    y_ref[...] = jnp.zeros_like(y_ref)
    pick = pick_ref[...]
    part = PS * QROWS
    for e in range(2):
        for b in range(LH):
            block = jnp.concatenate(
                [t_ref[b + s, e * part : (e + 1) * part, :].astype(jnp.bfloat16) for s in range(LH)], 1
            )
            got = jnp.dot(block, pick, preferred_element_type=jnp.float32)
            for big in range(PS):
                y_ref[
                    big * LANES + b * INNER : big * LANES + (b + 1) * INNER, e * LANES : (e + 1) * LANES
                ] = got[big * QROWS : big * QROWS + INNER]
    h_ref[...] = y_ref[: PS * LANES, :].astype(jnp.bfloat16)

    def times_hankel(left):
        outs = [
            jnp.dot(left, h_ref[a * LANES : a * LANES + SPAN, :], preferred_element_type=jnp.float32)
            for a in range(LH)
        ]
        re = jnp.concatenate([o[:, :LANES] for o in outs], 1)
        im = jnp.concatenate([o[:, LANES:] for o in outs], 1)
        return re, im

    p_re, p_im = times_hankel(test_ref[...])
    straight = jnp.concatenate([p_re, p_im], 1)
    crossed = jnp.concatenate([p_im, -p_re], 1)
    gram = hermitian(straight, straight, crossed)
    root = eliminate(gram, False)
    ortho = spread(root, jnp.concatenate([p_re, -p_im], 1), jnp.concatenate([p_im, p_re], 1))
    gap = jnp.zeros((HALF - RANK, SPAN), jnp.float32)
    q_rows = jnp.concatenate([ortho[:, :SPAN], gap, ortho[:, SPAN:], gap], 0)
    q_left = q_rows.astype(jnp.bfloat16)
    mixed_re, mixed_im = times_hankel(q_left)
    c_re = mixed_re[:RANK] - mixed_im[HALF : HALF + RANK]
    c_im = mixed_im[:RANK] + mixed_re[HALF : HALF + RANK]
    coupled = jnp.concatenate([c_re, c_im], 1)
    damping = hermitian(coupled, coupled, jnp.concatenate([-c_im, c_re], 1))
    lane = lax.broadcasted_iota(jnp.int32, (RANK, LANES), 1)
    row = lax.broadcasted_iota(jnp.int32, (RANK, LANES), 0)
    diagonal = lane == row
    level = DAMP * jnp.sum(jnp.where(diagonal, damping, 0.0)) / RANK
    solved = eliminate(damping + jnp.where(diagonal, level, 0.0), True)
    coeffs = coupled - level * spread(solved, coupled, jnp.concatenate([-c_im, c_re], 1))
    f_re = coeffs[:, :SPAN].astype(jnp.bfloat16)
    f_im = coeffs[:, SPAN:].astype(jnp.bfloat16)
    gap16 = jnp.zeros((HALF - RANK, LANES), jnp.bfloat16)
    q_t = jnp.transpose(q_rows).astype(jnp.bfloat16)
    y_ref[...] = jnp.zeros_like(y_ref)
    for a in range(LH):
        at = slice(a * LANES, (a + 1) * LANES)
        left = jnp.concatenate([f_re[:, at], gap16, f_im[:, at], gap16], 0)
        right = jnp.concatenate([f_im[:, at], gap16, -f_re[:, at], gap16], 0)
        y_ref[a * LANES : a * LANES + SPAN, :] += jnp.dot(
            q_t, jnp.concatenate([left, right], 1), preferred_element_type=jnp.float32
        )
    t_ref[...] = jnp.zeros_like(t_ref)
    pick_t = pick_t_ref[...]
    for e in range(2):
        for b in range(LH):
            lines = jnp.concatenate(
                [
                    y_ref[
                        big * LANES + b * INNER : big * LANES + b * INNER + QROWS,
                        e * LANES : (e + 1) * LANES,
                    ]
                    for big in range(PS)
                ],
                0,
            )
            high = lines.astype(jnp.bfloat16)
            low = (lines - high.astype(jnp.float32)).astype(jnp.bfloat16)
            wide_lines = jnp.dot(
                jnp.concatenate([high, low], 1), pick_t, preferred_element_type=jnp.float32
            )
            for s in range(LH):
                t_ref[b + s, e * part : (e + 1) * part, :] += wide_lines[:, s * LANES : (s + 1) * LANES]
    for big in range(PS):
        total = jnp.zeros((rows_ea, LANES), jnp.float32)
        for q in range(INNER):
            off = q // LH * PS + q % LH
            piece = t_ref[big, pl.ds(q, rows_ea, stride=QROWS), :]
            total = total + (pltpu.roll(piece, off, 1) if off else piece)
        out_ref[big] = total * scale_ref[big]


def reduce_frequency(spectrum, test_rows):
    laid = jnp.transpose(spectrum, (2, 0, 1, 3)).reshape(PS, 2 * PS, PLANE)
    laid = jnp.pad(laid, ((0, 0), (0, 0), (0, LANES - PLANE)))
    pick = picker()
    pick_t = np.concatenate([pick.T, pick.T], 0)
    out = pl.pallas_call(
        frequency_kernel,
        name="frequency",
        out_shape=jax.ShapeDtypeStruct((PS, 2 * PS, LANES), jnp.float32),
        in_specs=[pl.BlockSpec(memory_space=pltpu.VMEM)] * 5,
        out_specs=pl.BlockSpec(memory_space=pltpu.VMEM),
        scratch_shapes=[
            pltpu.VMEM((PS, 2 * PS * QROWS, LANES), jnp.float32),
            pltpu.VMEM((PS * LANES + 8, 2 * LANES), jnp.float32),
            pltpu.VMEM((PS * LANES, 2 * LANES), jnp.bfloat16),
        ],
        compiler_params=pltpu.CompilerParams(vmem_limit_bytes=40 * 1024 * 1024),
    )(
        laid,
        test_rows,
        jnp.asarray(pick, jnp.bfloat16),
        jnp.asarray(pick_t, jnp.bfloat16),
        jnp.asarray(scale_table()),
    )
    return jnp.transpose(out[:, :, :PLANE].reshape(PS, 2, PS, PLANE), (1, 2, 0, 3)).reshape(2, PS, TR3)


def exchange(by, full_ref, edge_ref, own, far, send, recv, consume):
    count = lax.axis_size("wide")
    patches = lax.axis_size("patch")
    mine = lax.axis_index("wide")
    here = lax.axis_index("patch")
    core = lax.axis_index("sub")
    target_patch = lax.rem(here + by + patches, patches)
    source_patch = lax.rem(here - by + patches, patches)
    barrier = pltpu.get_barrier_semaphore()
    mesh_ids = pl.DeviceIdType.MESH
    pl.semaphore_signal(barrier, inc=1, device_id={"sub": 1 - core}, device_id_type=mesh_ids)
    for k in range(count):
        other = lax.rem(mine + k, count)
        if k:
            pl.semaphore_signal(barrier, inc=1, device_id={"wide": other}, device_id_type=mesh_ids)
        pl.semaphore_signal(
            barrier, inc=1, device_id={"wide": other, "patch": source_patch}, device_id_type=mesh_ids
        )
    pl.semaphore_wait(barrier, 2 * count)

    def block(ref, index):
        return ref.at[core] if ref.shape[0] == 2 else ref.at[2 * index + core]

    def full_copy(target, slot):
        return pltpu.make_async_remote_copy(
            src_ref=block(full_ref, target),
            dst_ref=own.at[slot],
            send_sem=send.at[0, target],
            recv_sem=recv.at[0, slot],
            device_id={"wide": target},
            device_id_type=mesh_ids,
        )

    def edge_copy(target, slot):
        return pltpu.make_async_remote_copy(
            src_ref=block(edge_ref, target),
            dst_ref=far.at[slot],
            send_sem=send.at[1, target],
            recv_sem=recv.at[1, slot],
            device_id={"wide": target, "patch": target_patch},
            device_id_type=mesh_ids,
        )

    order = list(range(count - 1, -1, -1))
    for k in order:
        target = lax.rem(mine + k, count)
        if k:
            full_copy(target, mine).start()
        edge_copy(target, mine).start()
    own[mine] = block(full_ref, mine)[...]
    for k in order[::-1]:
        source = lax.rem(mine + count - k, count)
        if k:
            full_copy(source, source).wait_recv()
        edge_copy(source, source).wait_recv()
        consume(source)
    for k in order:
        target = lax.rem(mine + k, count)
        if k:
            full_copy(target, mine).wait_send()
        edge_copy(target, mine).wait_send()


def to_mate(source, target, send_sem, recv_sem):
    return pltpu.make_async_remote_copy(
        src_ref=source,
        dst_ref=target,
        send_sem=send_sem,
        recv_sem=recv_sem,
        device_id={"sub": 1 - lax.axis_index("sub")},
        device_id_type=pl.DeviceIdType.MESH,
    )


def collect_kernel(full_ref, edge_ref, own_out, far_out, own, far, send, recv, stage, mate, mate_send, mate_recv):
    core = lax.axis_index("sub")
    margin = far.shape[-1]
    traces = own.shape[-1]
    exchange(-1, full_ref, edge_ref, own, far, send, recv, lambda source: None)
    stage[0, :, :traces] = jnp.sum(own[...], 0).astype(jnp.bfloat16).astype(jnp.float32)
    stage[1] = jnp.zeros_like(stage[1])
    stage[1, :, :margin] = jnp.sum(far[...], 0).astype(jnp.bfloat16).astype(jnp.float32)
    copies = [to_mate(stage.at[i], mate.at[i], mate_send.at[i], mate_recv.at[i]) for i in range(2)]
    for copy in copies:
        copy.start()
    own_out[pl.ds(core, 1), :] = stage[0, :, :traces]
    far_out[pl.ds(core, 1), :] = stage[1, :, :margin]
    for copy in copies:
        copy.wait()
    own_out[pl.ds(1 - core, 1), :] = mate[0, :, :traces]
    far_out[pl.ds(1 - core, 1), :] = mate[1, :, :margin]


def share_kernel(full_ref, edge_ref, out_ref, own, far, send, recv, stage, mate, mate_send, mate_recv):
    core = lax.axis_index("sub")
    count = lax.axis_size("wide")
    width = far.shape[-1]

    def mate_copy(slot):
        return to_mate(stage.at[slot], mate.at[slot], mate_send.at[slot], mate_recv.at[slot])

    def consume(slot):
        stage[slot] = own[slot]
        stage[slot, :, :width] = own[slot, :, :width] + far[slot]
        mate_copy(slot).start()
        out_ref[pl.ds(2 * slot + core, 1), :] = stage[slot]

    exchange(1, full_ref, edge_ref, own, far, send, recv, consume)
    for slot in range(count):
        mate_copy(slot).wait()
        out_ref[pl.ds(2 * slot + 1 - core, 1), :] = mate[slot]


def exchange_call(kernel, name, full, edge, outs, slots, identity):
    count = lax.axis_size("wide")
    traces = full.shape[-1]
    return pl.pallas_call(
        kernel,
        name=name,
        out_shape=[jax.ShapeDtypeStruct(o, jnp.float32) for o in outs],
        in_specs=[pl.BlockSpec(memory_space=pltpu.VMEM)] * 2,
        out_specs=[pl.BlockSpec(memory_space=pltpu.VMEM)] * len(outs),
        scratch_shapes=[
            pltpu.VMEM((count, 1, traces), jnp.float32),
            pltpu.VMEM((count, 1, edge.shape[-1]), jnp.float32),
            pltpu.SemaphoreType.DMA((2, count)),
            pltpu.SemaphoreType.DMA((2, count)),
            pltpu.VMEM((slots, 1, traces), jnp.float32),
            pltpu.VMEM((slots, 1, traces), jnp.float32),
            pltpu.SemaphoreType.DMA((slots,)),
            pltpu.SemaphoreType.DMA((slots,)),
        ],
        compiler_params=pltpu.CompilerParams(
            collective_id=identity, has_side_effects=True, vmem_limit_bytes=40 * 1024 * 1024
        ),
    )(full, edge)


def shards(survey, test_matrix):
    wide_count = lax.axis_size("wide")
    mine = lax.axis_index("wide")
    time_local, plane_count, unused_size = survey.shape
    time_total = time_local * wide_count
    freq_total = FD * wide_count
    traces = plane_count * TR3
    margin = (LH - 1) * TR3
    forward = forward_table(time_total, freq_total)
    own_forward = lax.dynamic_slice_in_dim(forward, mine * time_local, time_local, 1)
    partial = jnp.dot(own_forward, survey.reshape(time_local, traces), preferred_element_type=jnp.float32)
    partial = partial.reshape(2 * freq_total, 1, traces)
    spectra, rim = exchange_call(
        collect_kernel, "collect", partial, partial[:, :, :margin], [(2 * FD, traces), (2 * FD, margin)], 2, 0
    )
    grid = jnp.concatenate([spectra, rim], 1).reshape(FD, 2, PS, PS, PLANE)
    test_rows = jnp.pad(
        test_matrix.T.reshape(RANK, LH, LH * INNER), ((0, 0), (0, 0), (0, LANES - LH * INNER))
    ).reshape(RANK, SPAN)
    smooth = jnp.stack([reduce_frequency(grid[f], test_rows) for f in range(FD)], 0)
    smooth = smooth.reshape(2 * FD, 1, PS * TR3)
    (gathered,) = exchange_call(
        share_kernel,
        "share",
        smooth[:, :, :traces],
        smooth[:, :, traces:],
        [(2 * freq_total, traces)],
        wide_count,
        1,
    )
    inverse = inverse_table(time_total, freq_total)
    own_inverse = lax.dynamic_slice_in_dim(inverse, mine * time_local, time_local, 1)
    series = lax.dot_general(
        own_inverse,
        gathered,
        (((0,), (0,)), ((), ())),
        precision=HIGHEST,
        preferred_element_type=jnp.float32,
    )
    return series.reshape(time_local, plane_count, TR3)


def solution(mesh):
    return jax.shard_map(
        shards,
        mesh=mesh,
        in_specs=(P("wide", ("grp", "patch"), None), P()),
        out_specs=P("wide", ("grp", "patch"), None),
        check_vma=False,
    )
```

```python
import functools
import math

import jax
import jax.numpy as jnp
import numpy as np
from jax import lax
from jax.experimental import pallas as pl
from jax.experimental.pallas import tpu as pltpu
from jax.sharding import PartitionSpec as P

LH = 5
RANK = 48
FD = 1
PS = 9
TR3 = 729
INNER = LH * LH
PLANE = PS * PS
DAMP = 0.5
HIGHEST = lax.Precision.HIGHEST
LANES = 128
HALF = 64
SPAN = LH * LANES
QROWS = 32


def level_weight():
    planes = np.arange(PS)
    return np.minimum(np.minimum(planes + 1, PS - planes), LH).astype(np.float32)


def tables(time_total, freq_total):
    turned = np.outer(np.arange(freq_total) + 1, np.arange(time_total)) % time_total
    angles = turned * (2.0 * math.pi / time_total)
    waves = np.stack([np.cos(angles), -np.sin(angles)], 1).reshape(2 * freq_total, time_total)
    forward = (waves / math.sqrt(time_total)).astype(np.float32)
    inverse = (waves * (2.0 / math.sqrt(time_total))).astype(np.float32)
    high = inverse.astype(jnp.bfloat16)
    low = (inverse - high.astype(np.float32)).astype(jnp.bfloat16)
    return forward.astype(jnp.bfloat16), np.concatenate([high, low, high], 0)


def picker():
    table = np.zeros((SPAN, LANES), np.float32)
    for b in range(LH):
        for c in range(LH):
            for d in range(LH):
                table[b * LANES + c * PS + d, b * INNER + c * LH + d] = 1.0
    return table


def scale_table():
    w = level_weight()
    taper = w / LH
    full = taper[None, :, None, None] / (
        w[:, None, None, None] * w[None, :, None, None] * w[None, None, :, None] * w[None, None, None, :]
    )
    full = full.reshape(PS, PS, PLANE)
    both = np.concatenate([full, full], 1)
    return np.pad(both, ((0, 0), (0, 0), (0, LANES - PLANE))).astype(np.float32)


def eliminate(matrix, full):
    groups = RANK // 8
    lane = lax.broadcasted_iota(jnp.int32, (8, LANES), 1)
    sub = lax.broadcasted_iota(jnp.int32, (8, LANES), 0)
    sign = jnp.where(lax.broadcasted_iota(jnp.int32, (1, LANES), 1) < HALF, -1.0, 1.0)
    x = [matrix[8 * g : 8 * g + 8] for g in range(groups)]
    w = [jnp.where(lane == sub + 8 * g, 1.0, 0.0) for g in range(groups)]
    inverses = []
    for k in range(RANK):
        home, at = divmod(k, 8)
        row_x = x[home][at : at + 1]
        row_w = w[home][at : at + 1]
        first = 0 if full else home
        m_re = {g: jnp.broadcast_to(x[g][:, k : k + 1], (8, LANES)) for g in range(first, groups)}
        m_im = {
            g: jnp.broadcast_to(x[g][:, HALF + k : HALF + k + 1], (8, LANES)) for g in range(first, groups)
        }
        turn_x = pltpu.roll(row_x, HALF, 1) * sign
        turn_w = pltpu.roll(row_w, HALF, 1) * sign
        inv = 1.0 / m_re[home][at : at + 1]
        inverses.append(inv)
        row_x = row_x * inv
        row_w = row_w * inv
        turn_x = turn_x * inv
        turn_w = turn_w * inv
        for g in range(first, groups):
            new_x = x[g] - (m_re[g] * row_x + m_im[g] * turn_x)
            new_w = w[g] - (m_re[g] * row_w + m_im[g] * turn_w)
            if g == home:
                keep = sub == at if full else sub <= at
                new_x = jnp.where(keep, x[g], new_x)
                new_w = jnp.where(keep, w[g], new_w)
            x[g] = new_x
            w[g] = new_w
    scale = []
    for g in range(groups):
        column = jnp.zeros((8, LANES), jnp.float32)
        for at in range(8):
            column = jnp.where(sub == at, inverses[8 * g + at], column)
        scale.append(column if full else jnp.sqrt(column))
    return jnp.concatenate([w[g] * scale[g] for g in range(groups)], 0)


def hermitian(left, re, im):
    gap = jnp.zeros((HALF - RANK, 2 * SPAN), jnp.float32)
    right = jnp.concatenate([re, gap, im, gap], 0)
    return lax.dot_general(
        left, right, (((1,), (1,)), ((), ())), precision=HIGHEST, preferred_element_type=jnp.float32
    )


def spread(left, top, bottom):
    gap = jnp.zeros((HALF - RANK, 2 * SPAN), jnp.float32)
    right = jnp.concatenate([top, gap, bottom, gap], 0)
    return jnp.dot(left, right, precision=HIGHEST, preferred_element_type=jnp.float32)


def frequency_kernel(x_ref, test_ref, pick_ref, pick_t_ref, scale_ref, out_ref, t_ref, y_ref, h_ref):
    rows_ea = 2 * PS
    t_ref[...] = jnp.zeros_like(t_ref)
    for q in range(INNER):
        off = q // LH * PS + q % LH
        for big in range(PS):
            piece = x_ref[big]
            if off:
                piece = pltpu.roll(piece, LANES - off, 1)
            t_ref[big, pl.ds(q, rows_ea, stride=QROWS), :] = piece
    y_ref[...] = jnp.zeros_like(y_ref)
    pick = pick_ref[...]
    part = PS * QROWS
    for e in range(2):
        for b in range(LH):
            block = jnp.concatenate(
                [t_ref[b + s, e * part : (e + 1) * part, :].astype(jnp.bfloat16) for s in range(LH)], 1
            )
            got = jnp.dot(block, pick, preferred_element_type=jnp.float32)
            for big in range(PS):
                y_ref[
                    big * LANES + b * INNER : big * LANES + (b + 1) * INNER, e * LANES : (e + 1) * LANES
                ] = got[big * QROWS : big * QROWS + INNER]
    h_ref[...] = y_ref[: PS * LANES, :].astype(jnp.bfloat16)

    def times_hankel(left):
        outs = [
            jnp.dot(left, h_ref[a * LANES : a * LANES + SPAN, :], preferred_element_type=jnp.float32)
            for a in range(LH)
        ]
        re = jnp.concatenate([o[:, :LANES] for o in outs], 1)
        im = jnp.concatenate([o[:, LANES:] for o in outs], 1)
        return re, im

    p_re, p_im = times_hankel(test_ref[...])
    straight = jnp.concatenate([p_re, p_im], 1)
    crossed = jnp.concatenate([p_im, -p_re], 1)
    gram = hermitian(straight, straight, crossed)
    root = eliminate(gram, False)
    ortho = spread(root, jnp.concatenate([p_re, -p_im], 1), jnp.concatenate([p_im, p_re], 1))
    gap = jnp.zeros((HALF - RANK, SPAN), jnp.float32)
    q_rows = jnp.concatenate([ortho[:, :SPAN], gap, ortho[:, SPAN:], gap], 0)
    q_left = q_rows.astype(jnp.bfloat16)
    mixed_re, mixed_im = times_hankel(q_left)
    c_re = mixed_re[:RANK] - mixed_im[HALF : HALF + RANK]
    c_im = mixed_im[:RANK] + mixed_re[HALF : HALF + RANK]
    coupled = jnp.concatenate([c_re, c_im], 1)
    damping = hermitian(coupled, coupled, jnp.concatenate([-c_im, c_re], 1))
    lane = lax.broadcasted_iota(jnp.int32, (RANK, LANES), 1)
    row = lax.broadcasted_iota(jnp.int32, (RANK, LANES), 0)
    diagonal = lane == row
    level = DAMP * jnp.sum(jnp.where(diagonal, damping, 0.0)) / RANK
    solved = eliminate(damping + jnp.where(diagonal, level, 0.0), True)
    coeffs = coupled - level * spread(solved, coupled, jnp.concatenate([-c_im, c_re], 1))
    f_re = coeffs[:, :SPAN].astype(jnp.bfloat16)
    f_im = coeffs[:, SPAN:].astype(jnp.bfloat16)
    gap16 = jnp.zeros((HALF - RANK, LANES), jnp.bfloat16)
    q_t = jnp.transpose(q_rows).astype(jnp.bfloat16)
    y_ref[...] = jnp.zeros_like(y_ref)
    for a in range(LH):
        at = slice(a * LANES, (a + 1) * LANES)
        left = jnp.concatenate([f_re[:, at], gap16, f_im[:, at], gap16], 0)
        right = jnp.concatenate([f_im[:, at], gap16, -f_re[:, at], gap16], 0)
        y_ref[a * LANES : a * LANES + SPAN, :] += jnp.dot(
            q_t, jnp.concatenate([left, right], 1), preferred_element_type=jnp.float32
        )
    t_ref[...] = jnp.zeros_like(t_ref)
    pick_t = pick_t_ref[...]
    for e in range(2):
        for b in range(LH):
            lines = jnp.concatenate(
                [
                    y_ref[
                        big * LANES + b * INNER : big * LANES + b * INNER + QROWS,
                        e * LANES : (e + 1) * LANES,
                    ]
                    for big in range(PS)
                ],
                0,
            )
            high = lines.astype(jnp.bfloat16)
            low = (lines - high.astype(jnp.float32)).astype(jnp.bfloat16)
            wide_lines = jnp.dot(
                jnp.concatenate([high, low], 1), pick_t, preferred_element_type=jnp.float32
            )
            for s in range(LH):
                t_ref[b + s, e * part : (e + 1) * part, :] += wide_lines[:, s * LANES : (s + 1) * LANES]
    for big in range(PS):
        total = jnp.zeros((rows_ea, LANES), jnp.float32)
        for q in range(INNER):
            off = q // LH * PS + q % LH
            piece = t_ref[big, pl.ds(q, rows_ea, stride=QROWS), :]
            total = total + (pltpu.roll(piece, off, 1) if off else piece)
        out_ref[big] = total * scale_ref[big]


def reduce_frequency(spectrum, test_rows):
    laid = jnp.transpose(spectrum, (2, 0, 1, 3)).reshape(PS, 2 * PS, PLANE)
    laid = jnp.pad(laid, ((0, 0), (0, 0), (0, LANES - PLANE)))
    pick = picker()
    pick_t = np.concatenate([pick.T, pick.T], 0)
    out = pl.pallas_call(
        frequency_kernel,
        name="frequency",
        out_shape=jax.ShapeDtypeStruct((PS, 2 * PS, LANES), jnp.float32),
        in_specs=[pl.BlockSpec(memory_space=pltpu.VMEM)] * 5,
        out_specs=pl.BlockSpec(memory_space=pltpu.VMEM),
        scratch_shapes=[
            pltpu.VMEM((PS, 2 * PS * QROWS, LANES), jnp.float32),
            pltpu.VMEM((PS * LANES + 8, 2 * LANES), jnp.float32),
            pltpu.VMEM((PS * LANES, 2 * LANES), jnp.bfloat16),
        ],
        compiler_params=pltpu.CompilerParams(vmem_limit_bytes=40 * 1024 * 1024),
    )(
        laid,
        test_rows,
        jnp.asarray(pick, jnp.bfloat16),
        jnp.asarray(pick_t, jnp.bfloat16),
        jnp.asarray(scale_table()),
    )
    return jnp.transpose(out[:, :, :PLANE].reshape(PS, 2, PS, PLANE), (1, 2, 0, 3)).reshape(2, PS, TR3)


def exchange(by, full_ref, edge_ref, own, far, send, recv, consume):
    count = lax.axis_size("wide")
    patches = lax.axis_size("patch")
    mine = lax.axis_index("wide")
    here = lax.axis_index("patch")
    core = lax.axis_index("sub")
    target_patch = lax.rem(here + by + patches, patches)
    source_patch = lax.rem(here - by + patches, patches)
    barrier = pltpu.get_barrier_semaphore()
    mesh_ids = pl.DeviceIdType.MESH
    pl.semaphore_signal(barrier, inc=1, device_id={"sub": 1 - core}, device_id_type=mesh_ids)
    for k in range(count):
        other = lax.rem(mine + k, count)
        if k:
            pl.semaphore_signal(barrier, inc=1, device_id={"wide": other}, device_id_type=mesh_ids)
        pl.semaphore_signal(
            barrier, inc=1, device_id={"wide": other, "patch": source_patch}, device_id_type=mesh_ids
        )
    pl.semaphore_wait(barrier, 2 * count)

    def block(ref, index):
        return ref.at[core] if ref.shape[0] == 2 else ref.at[2 * index + core]

    def full_copy(target, slot):
        return pltpu.make_async_remote_copy(
            src_ref=block(full_ref, target),
            dst_ref=own.at[slot],
            send_sem=send.at[0, target],
            recv_sem=recv.at[0, slot],
            device_id={"wide": target},
            device_id_type=mesh_ids,
        )

    def edge_copy(target, slot):
        return pltpu.make_async_remote_copy(
            src_ref=block(edge_ref, target),
            dst_ref=far.at[slot],
            send_sem=send.at[1, target],
            recv_sem=recv.at[1, slot],
            device_id={"wide": target, "patch": target_patch},
            device_id_type=mesh_ids,
        )

    order = list(range(count - 1, -1, -1))
    for k in order:
        target = lax.rem(mine + k, count)
        if k:
            full_copy(target, mine).start()
        edge_copy(target, mine).start()
    own[mine] = block(full_ref, mine)[...]
    for k in order[::-1]:
        source = lax.rem(mine + count - k, count)
        if k:
            full_copy(source, source).wait_recv()
        edge_copy(source, source).wait_recv()
        consume(source)
    for k in order:
        target = lax.rem(mine + k, count)
        if k:
            full_copy(target, mine).wait_send()
        edge_copy(target, mine).wait_send()


def to_mate(source, target, send_sem, recv_sem):
    return pltpu.make_async_remote_copy(
        src_ref=source,
        dst_ref=target,
        send_sem=send_sem,
        recv_sem=recv_sem,
        device_id={"sub": 1 - lax.axis_index("sub")},
        device_id_type=pl.DeviceIdType.MESH,
    )


def collect_kernel(
    full_ref, edge_ref, own_out, far_out, own, far, send, recv, stage, mate, mate_send, mate_recv, rows
):
    core = lax.axis_index("sub")
    margin = far.shape[-1]
    traces = own.shape[-1]
    exchange(-1, full_ref, edge_ref, own, far, send, recv, lambda source: None)
    stage[0, :, :traces] = jnp.sum(own[...], 0).astype(jnp.bfloat16).astype(jnp.float32)
    stage[1] = jnp.zeros_like(stage[1])
    stage[1, :, :margin] = jnp.sum(far[...], 0).astype(jnp.bfloat16).astype(jnp.float32)
    copies = [to_mate(stage.at[i], mate.at[i], mate_send.at[i], mate_recv.at[i]) for i in range(2)]
    for copy in copies:
        copy.start()
    own_out[pl.ds(core, 1), :] = stage[0, :, :traces]
    far_out[pl.ds(core, 1), :] = stage[1, :, :margin]
    for copy in copies:
        copy.wait()
    own_out[pl.ds(1 - core, 1), :] = mate[0, :, :traces]
    far_out[pl.ds(1 - core, 1), :] = mate[1, :, :margin]


def share_kernel(full_ref, edge_ref, out_ref, own, far, send, recv, stage, mate, mate_send, mate_recv, rows):
    core = lax.axis_index("sub")
    count = lax.axis_size("wide")
    width = far.shape[-1]

    def mate_copy(slot):
        return to_mate(stage.at[slot], mate.at[slot], mate_send.at[slot], mate_recv.at[slot])

    def consume(slot):
        stage[slot] = own[slot]
        stage[slot, :, :width] = own[slot, :, :width] + far[slot]
        mate_copy(slot).start()
        rows[pl.ds(2 * slot + core, 1), :] = stage[slot]

    exchange(1, full_ref, edge_ref, own, far, send, recv, consume)
    for slot in range(count):
        mate_copy(slot).wait()
        rows[pl.ds(2 * slot + 1 - core, 1), :] = mate[slot]
    exact = rows[...]
    high = exact.astype(jnp.bfloat16).astype(jnp.float32)
    out_ref[...] = jnp.concatenate([high, high, exact - high], 0).astype(jnp.bfloat16)


def exchange_call(kernel, name, full, edge, outs, slots, identity):
    count = lax.axis_size("wide")
    traces = full.shape[-1]
    return pl.pallas_call(
        kernel,
        name=name,
        out_shape=[jax.ShapeDtypeStruct(*o) for o in outs],
        in_specs=[pl.BlockSpec(memory_space=pltpu.VMEM)] * 2,
        out_specs=[pl.BlockSpec(memory_space=pltpu.VMEM)] * len(outs),
        scratch_shapes=[
            pltpu.VMEM((count, 1, traces), jnp.float32),
            pltpu.VMEM((count, 1, edge.shape[-1]), jnp.float32),
            pltpu.SemaphoreType.DMA((2, count)),
            pltpu.SemaphoreType.DMA((2, count)),
            pltpu.VMEM((slots, 1, traces), jnp.float32),
            pltpu.VMEM((slots, 1, traces), jnp.float32),
            pltpu.SemaphoreType.DMA((slots,)),
            pltpu.SemaphoreType.DMA((slots,)),
            pltpu.VMEM((2 * slots, traces), jnp.float32),
        ],
        compiler_params=pltpu.CompilerParams(
            collective_id=identity, has_side_effects=True, vmem_limit_bytes=40 * 1024 * 1024
        ),
    )(full, edge)


def shards(survey, test_matrix):
    wide_count = lax.axis_size("wide")
    mine = lax.axis_index("wide")
    time_local, plane_count, unused_size = survey.shape
    time_total = time_local * wide_count
    freq_total = FD * wide_count
    traces = plane_count * TR3
    margin = (LH - 1) * TR3
    forward, inverse = (jnp.asarray(table) for table in tables(time_total, freq_total))
    own_forward = lax.dynamic_slice_in_dim(forward, mine * time_local, time_local, 1)
    partial = lax.dot_general(
        own_forward, survey, (((1,), (0,)), ((), ())), preferred_element_type=jnp.float32
    )
    partial = partial.reshape(2 * freq_total, 1, traces)
    spectra, rim = exchange_call(
        collect_kernel, "collect", partial, partial[:, :, :margin], [((2 * FD, traces), jnp.float32), ((2 * FD, margin), jnp.float32)], 2, 0
    )
    grid = jnp.concatenate([spectra, rim], 1).reshape(FD, 2, PS, PS, PLANE)
    test_rows = jnp.pad(
        test_matrix.T.reshape(RANK, LH, LH * INNER), ((0, 0), (0, 0), (0, LANES - LH * INNER))
    ).reshape(RANK, SPAN)
    smooth = jnp.stack([reduce_frequency(grid[f], test_rows) for f in range(FD)], 0)
    smooth = smooth.reshape(2 * FD, 1, PS * TR3)
    (gathered,) = exchange_call(
        share_kernel,
        "share",
        smooth[:, :, :traces],
        smooth[:, :, traces:],
        [((6 * freq_total, traces), jnp.bfloat16)],
        wide_count,
        1,
    )
    own_inverse = lax.dynamic_slice_in_dim(inverse, mine * time_local, time_local, 1)
    return lax.dot_general(
        own_inverse,
        gathered.reshape(6 * freq_total, plane_count, TR3),
        (((0,), (0,)), ((), ())),
        preferred_element_type=jnp.float32,
    )


def solution(mesh):
    return jax.shard_map(
        shards,
        mesh=mesh,
        in_specs=(P("wide", ("grp", "patch"), None), P()),
        out_specs=P("wide", ("grp", "patch"), None),
        check_vma=False,
    )
```
